32 devices in a mesh: gx: 4 (over y, x), gy: 2 (over core), gz: 4 (over z).
Axes of the slice: x: 2, y: 2, z: 4, core: 2. Of those that a mesh axis runs over, the one named last changes fastest.
Arguments:
- fields: float32 [8, 96, 48, 1536], P(None, 'gx', 'gy', 'gz'), may hold values from -6 to 6
- new_owner: int32 [4, 2, 64], P('gx', 'gy', 'gz'), may hold values from 0 to 15, as said below
- new_slot: int32 [4, 2, 64], P('gx', 'gy', 'gz'), may hold values from 0 to 15, as said below
Outputs:
- indicator: float32 [96, 48, 1536], P('gx', 'gy', 'gz')
- new_blocks: float32 [4, 2, 64, 8, 20736], P('gx', 'gy', 'gz')
The draws below stay inside these ranges and needn't reach their ends.
Inputs may be any that keep to these rules, and one draw needn't show every extreme that they name: `new_owner`: the 16 old blocks of one device go to owners among the 16 devices of its gy index, exactly 1 of them to each owner. `new_slot`: the blocks that one owner receives have distinct slots.
All inputs are finite; a program needn't handle non-finite values.
Results may differ from the reference program's by a relative error of at most 0.00007.
Values sent between devices are 32-bit elements; how exact they have to be, the bound alone decides.
No kernel may reach another device: no remote copies, remote signals or barrier semaphores. Data moves between devices by JAX's collectives and lax.ppermute only.
A program may use at most 512 MiB of HBM per device.

```python
import jax
import jax.numpy as jnp
from jax import lax

F = 8
BS = 24
BZ = 16
NX = 96
NY = 48
NZ = 1536
N_GX = 4
N_GY = 2
N_GZ = 4


def remap_plan(key):
    group_size = N_GX * N_GZ
    capacity = BZ // group_size
    slots_total = group_size * capacity
    count_src = N_GX * N_GY * N_GZ
    source_keys = jax.random.split(jax.random.fold_in(key, 12), count_src)
    source_index = jnp.arange(count_src)
    source_row = source_index // N_GZ % N_GY
    source_local = source_index // (N_GY * N_GZ) * N_GZ + source_index % N_GZ

    def choose(one_key):
        return jax.random.permutation(one_key, BZ)
    picked = jax.vmap(choose)(source_keys)
    peers = picked // capacity
    copies = picked % capacity
    table_keys = jax.random.split(jax.random.fold_in(key, 13), count_src)
    tables = jax.vmap(lambda table_key: jax.random.permutation(table_key, slots_total))(table_keys)
    receiver = peers // N_GZ * (N_GY * N_GZ) + source_row[:, None] * N_GZ + peers % N_GZ
    slots = tables[receiver, source_local[:, None] * capacity + copies]
    shape = (N_GX, N_GY, N_GZ * BZ)
    return (peers.reshape(shape).astype(jnp.int32), slots.reshape(shape).astype(jnp.int32))


def draw_new_owner(key, part):
    owners, slots = remap_plan(key)
    return owners


def draw_new_slot(key, part):
    owners, slots = remap_plan(key)
    return slots


def block_scale(stream_key, shape, cuts, smallest, high):
    loudness = 1.0
    for dim, shards_of in cuts:
        draws = jax.random.uniform(jax.random.fold_in(jax.random.fold_in(stream_key, 6), dim), (shards_of,), jnp.float32, smallest / len(cuts), high / len(cuts))
        loudness = loudness * jnp.repeat(jnp.exp(draws), shape[dim] // shards_of).reshape((-1,) + (1,) * (len(shape) - 1 - dim))
    return loudness


def bell_draw(stream_key, extent, width, bound, cuts=(), kind=jnp.bfloat16):
    values = width * jax.random.normal(stream_key, extent, jnp.float32)
    if cuts:
        values = values * block_scale(stream_key, extent, cuts, -0.22, 0.18)
    return jnp.clip(values, -bound, bound).astype(kind)


def setup_inputs(seed: int = 0) -> dict:
    keys = jax.random.split(jax.random.key(seed), 4)
    fields = bell_draw(keys[0], (F, NX, NY, NZ), 1.0, 6.0, ((1, 4), (2, 2), (3, 4)), jnp.float32)
    new_owner = draw_new_owner(jax.random.fold_in(keys[3], 71), 0)
    new_slot = draw_new_slot(jax.random.fold_in(keys[3], 71), 0)
    return {"fields": fields, "new_owner": new_owner, "new_slot": new_slot}


filter_weight = 0.01
base_term = 0.1

def axis_terms(lower, center, upper):
    ahead = (upper - center) * 0.5
    behind = (center - lower) * 0.5
    second = (ahead - behind) * 0.5
    spread = jnp.abs(ahead) + jnp.abs(behind) + filter_weight * (jnp.abs(upper) + 2.0 * jnp.abs(center) + jnp.abs(lower)) + base_term
    return (second * second, spread * spread)

def reference(fields, new_owner, new_slot):

    def one_field(best, field):
        num_x, den_x = axis_terms(jnp.roll(field, 2, 0), field, jnp.roll(field, -2, 0))
        num_y, den_y = axis_terms(jnp.roll(field, 2, 1), field, jnp.roll(field, -2, 1))
        num_z, den_z = axis_terms(jnp.roll(field, 2, 2), field, jnp.roll(field, -2, 2))
        value = jnp.sqrt((num_x + num_y + num_z) / (den_x + den_y + den_z))
        return (jnp.maximum(best, value), None)
    start = jnp.zeros(fields.shape[1:], jnp.float32)
    indicator, unused = lax.scan(one_field, start, fields)
    group_size = N_GX * N_GZ
    capacity = BZ // group_size
    slots_total = group_size * capacity
    padded = jnp.pad(fields, ((0, 0), (2, 2), (2, 2), (2, 2)), mode='wrap')
    count_f = fields.shape[0]
    result = jnp.zeros((N_GX, N_GY, N_GZ * slots_total, count_f, BS * BS * BS + 12 * BS * BS), jnp.float32)
    total_blocks = N_GX * N_GY * N_GZ * BZ

    def place(index, result):
        index = jnp.asarray(index).astype(jnp.int32)
        block_x = index // (N_GY * N_GZ * BZ)
        block_y = index // (N_GZ * BZ) % N_GY
        block_z = index % (N_GZ * BZ)
        owner = new_owner[block_x, block_y, block_z].astype(jnp.int32)
        slot = new_slot[block_x, block_y, block_z].astype(jnp.int32)
        zero = jnp.zeros((), jnp.int32)
        cube = lax.dynamic_slice(padded, (zero, block_x * BS, block_y * BS, block_z * BS), (count_f, BS + 4, BS + 4, BS + 4))
        pieces = [cube[:, 2:-2, 2:-2, 2:-2], cube[:, 0:2, 2:-2, 2:-2], cube[:, -2:, 2:-2, 2:-2], cube[:, 2:-2, 0:2, 2:-2], cube[:, 2:-2, -2:, 2:-2], cube[:, 2:-2, 2:-2, 0:2], cube[:, 2:-2, 2:-2, -2:]]
        record = jnp.concatenate([piece.reshape(count_f, -1) for piece in pieces], axis=1)
        owner_x = owner // N_GZ
        owner_z = owner % N_GZ
        return lax.dynamic_update_slice(result, record[None, None, None], (owner_x, block_y, owner_z * slots_total + slot, zero, zero))
    new_blocks = lax.fori_loop(0, total_blocks, place, result)
    return (indicator, new_blocks)
```

```python
import functools

import jax
import jax.numpy as jnp
from jax import lax
from jax.experimental import pallas as pl
from jax.experimental.pallas import tpu as pltpu
from jax.sharding import PartitionSpec as P

BS = 24
WIDTH = 2
AHEAD = 4
FAR_WINDOW, NEAR_WINDOW = 2, 3
TAIL = 128
GROUP = ("gx", "gz")

filter_weight = 0.01
base_term = 0.1


def block_transpose(rows, count, lanes):
    depth = count * BS
    place = lanes // BS
    skewed = [rows[0]] + [pltpu.roll(rows[r], BS * r, 1) for r in range(1, count)]
    held = [skewed[-j % count] for j in range(count)]
    step = 1
    while step < count:
        moves = (place & step) != 0
        held = [jnp.where(moves, held[(j - step) % count], held[j]) for j in range(count)]
        step *= 2
    return [held[0]] + [pltpu.roll(held[k], depth - BS * k, 1) for k in range(1, count)]


def load_rows(ref, x, start):
    return jnp.swapaxes(ref[:, x, pl.ds(start, 8), :], 0, 1)


def offset_of(owner, me, size):
    return owner ^ me if size & (size - 1) == 0 else lax.rem(owner - me + size, size)


def core_kernel(wide, fields_ref, owner_ref, slot_ref, *refs):
    count = owner_ref.shape[-1]
    outs = refs[:count]
    x_low, x_high, y_low, y_high, cells, held, labels, owners, slots = refs[count:-3]
    in_sems, fetch_sems, out_sems = refs[-3:]
    me = lax.axis_index("gx") * lax.axis_size("gz") + lax.axis_index("gz")
    size = lax.axis_size("gx") * lax.axis_size("gz")
    count_f, side_x, side_y, depth = fields_ref.shape
    steps = side_x // wide
    part = wide * side_y * BS

    def load(step):
        planes = pl.ds(step * wide, wide)
        return pltpu.make_async_copy(fields_ref.at[:, planes], cells.at[:, planes], in_sems.at[step])

    def stores(step):
        slot = lax.rem(step, 2)
        at = pl.ds(pl.multiple_of(step * part, 128), part)
        return [
            pltpu.make_async_copy(held.at[slot, d], outs[d].at[:, at], out_sems.at[slot, d])
            for d in range(count)
        ]

    fetches = [
        pltpu.make_async_copy(owner_ref, owners, fetch_sems.at[0]),
        pltpu.make_async_copy(slot_ref, slots, fetch_sems.at[1]),
    ]
    for fetch in fetches:
        fetch.start()
    for step in range(steps):
        load(step).start()
    for fetch in fetches:
        fetch.wait()
    dests = [offset_of(owners[0, 0, k], me, size) for k in range(count)]
    for k in range(count):
        labels[dests[k]] = jnp.full((count_f, TAIL), slots[0, 0, k].astype(jnp.float32))
    tails = [
        pltpu.make_async_copy(
            labels.at[d], outs[d].at[:, pl.ds(outs[d].shape[1] - TAIL, TAIL)], out_sems.at[2, d]
        )
        for d in range(count)
    ]
    for tail in tails:
        tail.start()
    lanes = lax.broadcasted_iota(jnp.int32, (count_f, depth), 1)
    tiles = [(x, start) for x in range(wide) for start in range(0, side_y, 8)]
    per_group = count // 8

    def one_step(step, carry):
        load(step).wait()

        @pl.when(step > 1)
        def _():
            for copy in stores(step - 2):
                copy.wait()

        now = lax.rem(step, 2)
        for group in range(len(tiles) // per_group):
            rows = []
            for x, start in tiles[group * per_group : (group + 1) * per_group]:
                tile = load_rows(cells, step * wide + x, start)
                for r in range(8):
                    y = start + r
                    rows.append(tile[r])
                    if y < WIDTH:
                        y_low[(step * wide + x) * WIDTH + y] = tile[r]
                    if y >= side_y - WIDTH:
                        y_high[(step * wide + x) * WIDTH + y - (side_y - WIDTH)] = tile[r]
            for k, piece in enumerate(block_transpose(rows, count, lanes)):
                held[now, dests[k], :, pl.ds(group * depth, depth)] = piece
        for copy in stores(step):
            copy.start()
        return carry

    lax.fori_loop(0, steps, one_step, 0)
    for x in range(WIDTH):
        for start in range(0, side_y, 8):
            at = pl.ds(x * side_y + start, 8)
            x_low[at] = load_rows(cells, x, start)
            x_high[at] = load_rows(cells, side_x - WIDTH + x, start)
    for step in (steps - 2, steps - 1):
        for copy in stores(step):
            copy.wait()
    for tail in tails:
        tail.wait()


def edge_kernel(fields_ref, rows_ref, low_ref, high_ref, first_ref, last_ref, low_rows, high_rows):
    count_f, wide, side_y, depth = fields_ref.shape
    count = depth // BS
    lanes = lax.broadcasted_iota(jnp.int32, (count_f, depth), 1)
    slot = lanes % BS // WIDTH
    per = BS // WIDTH

    def one_x(x, carry):
        low = high = None
        for start in range(0, side_y, 8):
            tile = load_rows(fields_ref, x, start)
            rows_ref[x, pl.ds(start, 8)] = tile
            for r in range(8):
                y = start + r
                i = y % per
                moved = tile[r] if i == 0 else pltpu.roll(tile[r], WIDTH * i, 1)
                if i == 0:
                    high = low = moved
                else:
                    high = jnp.where(slot == i, moved, high)
                    low = jnp.where(slot == i - 1, moved, low)
                if i == per - 1:
                    high_rows[x * (side_y // per) + y // per] = high
                    low_rows[x * (side_y // per) + y // per] = pltpu.roll(low, WIDTH, 1)
        return carry

    lax.fori_loop(0, wide, one_x, 0)
    lows = block_transpose([low_rows[r] for r in range(count)], count, lanes)
    for k in range(count):
        low_ref[k] = lows[k]
    last_ref[...] = lows[0]
    highs = block_transpose([high_rows[r] for r in range(count)], count, lanes)
    for k in range(count):
        high_ref[(k - 1) % count] = highs[k]
    first_ref[...] = highs[0]


def halo_kernel(
    start, dest_ref, x_low, x_high, y_low, y_high, z_low, z_high, before_z, after_z, *refs
):
    count = dest_ref.shape[0]
    outs, held, sems = refs[-count - 2 : -2], refs[-2], refs[-1]
    row_count, count_f, depth = x_low.shape
    lanes = lax.broadcasted_iota(jnp.int32, (count_f, depth), 1)
    piece_len = row_count * BS
    for n, ref in enumerate((x_low, x_high, y_low, y_high)):

        def one_group(group, carry, ref=ref, n=n):
            rows = [ref[group * count + r] for r in range(count)]
            at = pl.multiple_of(n * piece_len + group * depth, 128)
            for k, piece in enumerate(block_transpose(rows, count, lanes)):
                held[dest_ref[k], :, pl.ds(at, depth)] = piece
            return carry

        lax.fori_loop(0, row_count // count, one_group, 0)
    for k in range(count):
        low = before_z[...] if k == 0 else z_low[k]
        high = after_z[...] if k == count - 1 else z_high[k]
        held[dest_ref[k], :, pl.ds(4 * piece_len, piece_len)] = low
        held[dest_ref[k], :, pl.ds(5 * piece_len, piece_len)] = high
    copies = []
    for d in range(count):
        length = held.shape[2]
        at = pl.ds(0 if outs[d].shape[1] == length else start, length)
        copies.append(pltpu.make_async_copy(held.at[d], outs[d].at[:, at], sems.at[d]))
        copies[d].start()
    for copy in copies:
        copy.wait()


def axis_terms(lower, center, upper):
    ahead = (upper - center) * 0.5
    behind = (center - lower) * 0.5
    second = (ahead - behind) * 0.5
    spread = (
        jnp.abs(ahead)
        + jnp.abs(behind)
        + filter_weight * (jnp.abs(upper) + 2.0 * jnp.abs(center) + jnp.abs(lower))
        + base_term
    )
    return (second * second, spread * spread)


def indicator_kernel(
    prev_ref, rows_ref, next_ref, y_low, y_high, before_z, after_z, *refs
):
    out_ref, held = refs[-2:]
    wide, side_y, count_f, depth = rows_ref.shape
    lanes = lax.broadcasted_iota(jnp.int32, (count_f, depth), 1)
    held[0:WIDTH] = prev_ref[...]
    held[WIDTH : WIDTH + wide] = rows_ref[...]
    held[WIDTH + wide :] = next_ref[...]

    def one_x(x, carry):
        shift = lax.rem(depth - x * (side_y * WIDTH), depth)
        before = pltpu.roll(before_z[...], shift, 1)
        after = pltpu.roll(after_z[...], shift, 1)
        for y in range(side_y):
            center = held[x + WIDTH, y]
            num, den = axis_terms(held[x, y], center, held[x + 2 * WIDTH, y])
            behind = y_low[x, y] if y < WIDTH else held[x + WIDTH, y - WIDTH]
            past = y + WIDTH - side_y
            ahead = y_high[x, past] if past >= 0 else held[x + WIDTH, y + WIDTH]
            num_y, den_y = axis_terms(behind, center, ahead)
            behind = jnp.where(
                lanes < WIDTH,
                pltpu.roll(before, depth - WIDTH * y, 1) if y else before,
                pltpu.roll(center, WIDTH, 1),
            )
            ahead = jnp.where(
                lanes >= depth - WIDTH,
                pltpu.roll(after, depth - WIDTH - WIDTH * y, 1),
                pltpu.roll(center, depth - WIDTH, 1),
            )
            num_z, den_z = axis_terms(behind, center, ahead)
            ratio = (num + num_y + num_z) / (den + den_y + den_z)
            out_ref[x, pl.ds(y, 1), :] = jnp.sqrt(jnp.max(ratio, axis=0, keepdims=True))
        return carry

    lax.fori_loop(0, wide, one_x, 0)


def place_kernel(count, has_base, *refs):
    arrays = refs[:count]
    out, slots = refs[count + has_base : count + has_base + 2]
    held, sems = refs[-count - 1 : -1], refs[-1]
    fetches = [pltpu.make_async_copy(arrays[n], held[n], sems.at[0, n]) for n in range(count)]
    for fetch in fetches:
        fetch.start()
    copies = []
    for n in range(count):
        length = arrays[n].shape[1] - TAIL
        fetches[n].wait()
        slot = jnp.max(held[n][:, pl.ds(length, TAIL)]).astype(jnp.int32)
        slots[n] = slot
        at = pl.ds(0, length)
        copies.append(
            pltpu.make_async_copy(held[n].at[:, at], out.at[slot, :, at], sems.at[1, n])
        )
        copies[n].start()
    for copy in copies:
        copy.wait()


def place(arrays, shape, base=None):
    count = len(arrays)
    has_base = 0 if base is None else 1
    hbm = pl.BlockSpec(memory_space=pltpu.HBM)
    return pl.pallas_call(
        functools.partial(place_kernel, count, has_base),
        out_shape=[
            jax.ShapeDtypeStruct(shape, jnp.float32),
            jax.ShapeDtypeStruct((count,), jnp.int32),
        ],
        in_specs=[pl.BlockSpec(memory_space=pl.ANY)] * count + [hbm] * has_base,
        out_specs=[hbm, pl.BlockSpec(memory_space=pltpu.SMEM)],
        scratch_shapes=[pltpu.VMEM(array.shape, jnp.float32) for array in arrays]
        + [pltpu.SemaphoreType.DMA((2, count))],
        input_output_aliases={count: 0} if has_base else {},
        compiler_params=pltpu.CompilerParams(vmem_limit_bytes=60 * 2**20),
    )(*arrays, *([base] if has_base else []))


def place_halos_kernel(start, count, slots_ref, *refs):
    arrays = refs[:count]
    out, sems = refs[count + 1 :]
    length = arrays[0].shape[1]
    copies = [
        pltpu.make_async_copy(arrays[n], out.at[slots_ref[n], :, pl.ds(start, length)], sems.at[n])
        for n in range(count)
    ]
    for copy in copies:
        copy.start()
    for copy in copies:
        copy.wait()


def place_halos(start, slots, arrays, placed):
    count = len(arrays)
    hbm = pl.BlockSpec(memory_space=pltpu.HBM)
    return pl.pallas_call(
        functools.partial(place_halos_kernel, start, count),
        out_shape=jax.ShapeDtypeStruct(placed.shape, jnp.float32),
        in_specs=[pl.BlockSpec(memory_space=pltpu.SMEM)]
        + [pl.BlockSpec(memory_space=pltpu.VMEM)] * count
        + [hbm],
        out_specs=hbm,
        scratch_shapes=[pltpu.SemaphoreType.DMA((count,))],
        input_output_aliases={1 + count: 0},
        compiler_params=pltpu.CompilerParams(vmem_limit_bytes=12 * 2**20),
    )(slots, *arrays, placed)


def send_order(width_x, width_z):
    xs = [0, 3, 1, 2] if width_x == 4 else list(range(width_x))
    half = width_z // 2
    far = [x * width_z + z for x in xs for z in reversed(range(half, width_z))]
    near = [x * width_z + z for x in reversed(range(width_x)) for z in reversed(range(half))]
    return far, [d for d in near if d]


def ring(axis, move):
    size = lax.axis_size(axis)
    return [(i, (i + move) % size) for i in range(size)]


def per_device(fields, new_owner, new_slot):
    count_f, side_x, side_y, depth = fields.shape
    count = depth // BS
    width_x, width_z = lax.axis_size("gx"), lax.axis_size("gz")
    size = width_x * width_z
    is_power = size & (size - 1) == 0
    me = lax.axis_index(GROUP).astype(jnp.int32)
    dest = offset_of(new_owner.reshape(count), me, size)

    far, near = send_order(width_x, width_z)
    split = far[:AHEAD]
    core_len = side_x * side_y * BS
    halo_len = 12 * BS * side_y
    wide = 4
    part = wide * side_y * BS
    halo_rows = WIDTH * side_y
    row_shape = jax.ShapeDtypeStruct((halo_rows, count_f, depth), jnp.float32)
    hbm = pl.BlockSpec(memory_space=pltpu.HBM)
    whole = pl.BlockSpec(memory_space=pltpu.VMEM)
    *core, x_first, x_last, y_first, y_last = pl.pallas_call(
        functools.partial(core_kernel, wide),
        out_shape=[
            jax.ShapeDtypeStruct(
                (count_f, core_len + (0 if d in split else halo_len) + TAIL), jnp.float32
            )
            for d in range(count)
        ]
        + [row_shape] * 4,
        in_specs=[hbm, hbm, hbm],
        out_specs=[hbm] * count + [whole] * 4,
        scratch_shapes=[
            pltpu.VMEM(fields.shape, jnp.float32),
            pltpu.VMEM((2, count, count_f, part), jnp.float32),
            pltpu.VMEM((count, count_f, TAIL), jnp.float32),
            pltpu.SMEM(new_owner.shape, jnp.int32),
            pltpu.SMEM(new_owner.shape, jnp.int32),
            pltpu.SemaphoreType.DMA((side_x // wide,)),
            pltpu.SemaphoreType.DMA((2,)),
            pltpu.SemaphoreType.DMA((3, count)),
        ],
        compiler_params=pltpu.CompilerParams(vmem_limit_bytes=60 * 2**20),
        cost_estimate=pl.CostEstimate(flops=0, bytes_accessed=32 * 2**20, transcendentals=0),
    )(fields, new_owner, new_slot)

    span = 8
    z_shape = jax.ShapeDtypeStruct((count, count_f, halo_rows * BS), jnp.float32)
    edge_shape = jax.ShapeDtypeStruct((count_f, halo_rows * BS), jnp.float32)
    z_block = pl.BlockSpec((count, count_f, depth), lambda i: (0, 0, i))
    edge_block = pl.BlockSpec((count_f, depth), lambda i: (0, i))
    rows_block = pl.BlockSpec((span, side_y, count_f, depth), lambda i: (i, 0, 0, 0))
    rows, z_low, z_high, z_first, z_last = pl.pallas_call(
        edge_kernel,
        out_shape=[
            jax.ShapeDtypeStruct((side_x, side_y, count_f, depth), jnp.float32),
            z_shape,
            z_shape,
            edge_shape,
            edge_shape,
        ],
        grid=(side_x // span,),
        in_specs=[pl.BlockSpec((count_f, span, side_y, depth), lambda i: (0, i, 0, 0))],
        out_specs=[rows_block, z_block, z_block, edge_block, edge_block],
        scratch_shapes=[pltpu.VMEM((count, count_f, depth), jnp.float32)] * 2,
        compiler_params=pltpu.CompilerParams(vmem_limit_bytes=60 * 2**20),
        cost_estimate=pl.CostEstimate(flops=0, bytes_accessed=32 * 2**20, transcendentals=0),
    )(fields)

    values = {("core", d): core[d] for d in split}
    values |= {"x_up": x_last, "x_down": x_first, "y_up": y_last, "y_down": y_first}
    values |= {"z_up": z_last, "z_down": z_first}
    arrived = {}

    def start(name, *after):
        value = values[name]
        if after:
            value, *_ = lax.optimization_barrier((value, *after))
        if isinstance(name, str):
            axis = "g" + name[0]
            pairs = ring(axis, 1 if name.endswith("up") else -1)
        else:
            axis, d = GROUP, name[1]
            move = (lambda s: s ^ d) if is_power else (lambda s: (s + d) % size)
            pairs = [(s, move(s)) for s in range(size)]
        arrived[name] = lax.ppermute(value, axis, pairs)

    far_chain, near_chain = [], []

    def start_far(name, *after):
        past = [arrived[far_chain[-FAR_WINDOW]]] if len(far_chain) >= FAR_WINDOW else []
        start(name, *past, *after)
        far_chain.append(name)

    def start_near(name, *after):
        past = [arrived[near_chain[-NEAR_WINDOW]]] if len(near_chain) >= NEAR_WINDOW else []
        start(name, *past, *after)
        near_chain.append(name)

    for d in split:
        start_far(("core", d))
    for name in ("x_up", "y_up", "x_down", "y_down", "z_up", "z_down"):
        start_near(name)
    x_low, x_high = arrived["x_up"], arrived["x_down"]
    y_low, y_high = arrived["y_up"], arrived["y_down"]
    before_z, after_z = arrived["z_up"], arrived["z_down"]

    full = [d for d in range(size) if d not in split]
    halos = pl.pallas_call(
        functools.partial(halo_kernel, core_len),
        out_shape=[
            jax.ShapeDtypeStruct((count_f, halo_len) if d in split else core[d].shape, jnp.float32)
            for d in range(count)
        ],
        in_specs=[pl.BlockSpec(memory_space=pltpu.SMEM)] + [whole] * 8 + [hbm] * len(full),
        out_specs=[hbm] * count,
        input_output_aliases={9 + n: d for n, d in enumerate(full)},
        scratch_shapes=[
            pltpu.VMEM((count, count_f, halo_len), jnp.float32),
            pltpu.SemaphoreType.DMA((count,)),
        ],
        compiler_params=pltpu.CompilerParams(vmem_limit_bytes=60 * 2**20),
        cost_estimate=pl.CostEstimate(flops=0, bytes_accessed=32 * 2**20, transcendentals=0),
    )(
        dest, x_low, x_high, y_low, y_high, z_low, z_high, before_z, after_z,
        *[core[d] for d in full],
    )
    parts = side_x // span
    per_span = span // WIDTH
    side_block = (WIDTH, side_y, count_f, depth)
    indicators = []
    for n in range(parts):

        def at(block, *index):
            return pl.BlockSpec(block, lambda i: index)

        prev, prev_at = (rows, n * per_span - 1) if n else (x_low.reshape(side_block), 0)
        last = n == parts - 1
        next, next_at = (x_high.reshape(side_block), 0) if last else (rows, (n + 1) * per_span)
        y_block = at((span, WIDTH, count_f, depth), n, 0, 0, 0)
        z_part = at((count_f, depth), 0, n)
        indicators.append(
            pl.pallas_call(
                indicator_kernel,
                out_shape=jax.ShapeDtypeStruct((side_x, side_y, depth), jnp.float32),
                grid=(1,),
                in_specs=[
                    at(side_block, prev_at, 0, 0, 0),
                    at((span, side_y, count_f, depth), n, 0, 0, 0),
                    at(side_block, next_at, 0, 0, 0),
                    y_block,
                    y_block,
                    z_part,
                    z_part,
                ]
                + [hbm] * (n > 0),
                out_specs=at((span, side_y, depth), n, 0, 0),
                scratch_shapes=[
                    pltpu.VMEM((span + 2 * WIDTH, side_y, count_f, depth), jnp.float32)
                ],
                input_output_aliases={7: 0} if n else {},
                compiler_params=pltpu.CompilerParams(vmem_limit_bytes=60 * 2**20),
                cost_estimate=pl.CostEstimate(
                    flops=10**8, bytes_accessed=16 * 2**20, transcendentals=0
                ),
            )(
                prev,
                rows,
                next,
                y_low.reshape(side_x, WIDTH, count_f, depth),
                y_high.reshape(side_x, WIDTH, count_f, depth),
                before_z,
                after_z,
                *indicators[-1:],
            )
        )

    values |= {("halo" if d in split else "all", d): halos[d] for d in range(size)}
    far_rest = [("all", d) for d in far[AHEAD:]] + [("halo", d) for d in split]
    beside = dict(zip(far_rest[len(far_rest) - parts - len(split) + 1 :], indicators))
    shape = (count, count_f, core_len + halo_len)
    placed, slots = place([arrived["core", d] for d in split], shape)
    beside[far_rest[-len(split) // 2]] = slots
    for name in far_rest:
        start_far(name, *([beside[name]] if name in beside else []))
    for d in near:
        start_near(("all", d))
    placed, _ = place([halos[0]] + [arrived["all", d] for d in full if d], shape, placed)
    placed = place_halos(core_len, slots, [arrived["halo", d] for d in split], placed)
    return (indicators[-1], placed.reshape((1, 1) + shape))


def solution(mesh):
    placed = (P(None, "gx", "gy", "gz"), P("gx", "gy", "gz"), P("gx", "gy", "gz"))
    return jax.shard_map(
        per_device,
        mesh=mesh,
        in_specs=placed,
        out_specs=(P("gx", "gy", "gz"), P("gx", "gy", "gz", None, None)),
        check_vma=False,
    )
```

```python
import functools

import jax
import jax.numpy as jnp
from jax import lax
from jax.experimental import pallas as pl
from jax.experimental.pallas import tpu as pltpu
from jax.sharding import PartitionSpec as P

BS = 24
WIDTH = 2
AHEAD = 3
FAR_WINDOW, NEAR_WINDOW = 2, 3
TAIL = 128
GROUP = ("gx", "gz")

filter_weight = 0.01
base_term = 0.1


def block_transpose(rows, count, lanes):
    depth = count * BS
    place = lanes // BS
    skewed = [rows[0]] + [pltpu.roll(rows[r], BS * r, 1) for r in range(1, count)]
    held = [skewed[-j % count] for j in range(count)]
    step = 1
    while step < count:
        moves = (place & step) != 0
        held = [jnp.where(moves, held[(j - step) % count], held[j]) for j in range(count)]
        step *= 2
    return [held[0]] + [pltpu.roll(held[k], depth - BS * k, 1) for k in range(1, count)]


def load_rows(ref, x, start):
    return jnp.swapaxes(ref[:, x, pl.ds(start, 8), :], 0, 1)


def offset_of(owner, me, size):
    return owner ^ me if size & (size - 1) == 0 else lax.rem(owner - me + size, size)


def core_kernel(wide, fields_ref, owner_ref, slot_ref, *refs):
    count = owner_ref.shape[-1]
    outs = refs[:count]
    x_low, x_high, y_ends, cells, held, labels, owners, slots = refs[count:-3]
    in_sems, fetch_sems, out_sems = refs[-3:]
    me = lax.axis_index("gx") * lax.axis_size("gz") + lax.axis_index("gz")
    size = lax.axis_size("gx") * lax.axis_size("gz")
    count_f, side_x, side_y, depth = fields_ref.shape
    steps = side_x // wide
    part = wide * side_y * BS

    def load(step):
        planes = pl.ds(step * wide, wide)
        return pltpu.make_async_copy(fields_ref.at[:, planes], cells.at[:, planes], in_sems.at[step])

    def stores(step):
        slot = lax.rem(step, 2)
        at = pl.ds(pl.multiple_of(step * part, 128), part)
        return [
            pltpu.make_async_copy(held.at[slot, d], outs[d].at[:, at], out_sems.at[slot, d])
            for d in range(count)
        ]

    fetches = [
        pltpu.make_async_copy(owner_ref, owners, fetch_sems.at[0]),
        pltpu.make_async_copy(slot_ref, slots, fetch_sems.at[1]),
    ]
    for fetch in fetches:
        fetch.start()
    for step in range(steps):
        load(step).start()
    for fetch in fetches:
        fetch.wait()
    dests = [offset_of(owners[0, 0, k], me, size) for k in range(count)]
    for k in range(count):
        labels[dests[k]] = jnp.full((count_f, TAIL), slots[0, 0, k].astype(jnp.float32))
    tails = [
        pltpu.make_async_copy(
            labels.at[d], outs[d].at[:, pl.ds(outs[d].shape[1] - TAIL, TAIL)], out_sems.at[2, d]
        )
        for d in range(count)
    ]
    for tail in tails:
        tail.start()
    lanes = lax.broadcasted_iota(jnp.int32, (count_f, depth), 1)
    tiles = [(x, start) for x in range(wide) for start in range(0, side_y, 8)]
    per_group = count // 8

    def one_step(step, carry):
        load(step).wait()

        @pl.when(step > 1)
        def _():
            for copy in stores(step - 2):
                copy.wait()

        now = lax.rem(step, 2)
        for group in range(len(tiles) // per_group):
            rows = []
            for x, start in tiles[group * per_group : (group + 1) * per_group]:
                tile = load_rows(cells, step * wide + x, start)
                for r in range(8):
                    y = start + r
                    rows.append(tile[r])
                    if y < WIDTH:
                        y_ends[1, (step * wide + x) * WIDTH + y] = tile[r]
                    if y >= side_y - WIDTH:
                        y_ends[0, (step * wide + x) * WIDTH + y - (side_y - WIDTH)] = tile[r]
            for k, piece in enumerate(block_transpose(rows, count, lanes)):
                held[now, dests[k], :, pl.ds(group * depth, depth)] = piece
        for copy in stores(step):
            copy.start()
        return carry

    lax.fori_loop(0, steps, one_step, 0)
    for x in range(WIDTH):
        for start in range(0, side_y, 8):
            at = pl.ds(x * side_y + start, 8)
            x_low[at] = load_rows(cells, x, start)
            x_high[at] = load_rows(cells, side_x - WIDTH + x, start)
    for step in (steps - 2, steps - 1):
        for copy in stores(step):
            copy.wait()
    for tail in tails:
        tail.wait()


def edge_kernel(fields_ref, rows_ref, low_ref, high_ref, first_ref, last_ref, low_rows, high_rows):
    count_f, wide, side_y, depth = fields_ref.shape
    count = depth // BS
    lanes = lax.broadcasted_iota(jnp.int32, (count_f, depth), 1)
    slot = lanes % BS // WIDTH
    per = BS // WIDTH

    def one_x(x, carry):
        low = high = None
        for start in range(0, side_y, 8):
            tile = load_rows(fields_ref, x, start)
            rows_ref[x, pl.ds(start, 8)] = tile
            for r in range(8):
                y = start + r
                i = y % per
                moved = tile[r] if i == 0 else pltpu.roll(tile[r], WIDTH * i, 1)
                if i == 0:
                    high = low = moved
                else:
                    high = jnp.where(slot == i, moved, high)
                    low = jnp.where(slot == i - 1, moved, low)
                if i == per - 1:
                    high_rows[x * (side_y // per) + y // per] = high
                    low_rows[x * (side_y // per) + y // per] = pltpu.roll(low, WIDTH, 1)
        return carry

    lax.fori_loop(0, wide, one_x, 0)
    lows = block_transpose([low_rows[r] for r in range(count)], count, lanes)
    for k in range(count):
        low_ref[k] = lows[k]
    last_ref[...] = lows[0]
    highs = block_transpose([high_rows[r] for r in range(count)], count, lanes)
    for k in range(count):
        high_ref[(k - 1) % count] = highs[k]
    first_ref[...] = highs[0]


def halo_kernel(
    start, sequence, dest_ref, x_low, x_high, y_halos, z_low, z_high, before_z, after_z, *refs
):
    count = dest_ref.shape[0]
    outs = {d: refs[n - count - 2] for n, d in enumerate(sequence)}
    held, sems = refs[-2:]
    row_count, count_f, depth = x_low.shape
    lanes = lax.broadcasted_iota(jnp.int32, (count_f, depth), 1)
    piece_len = row_count * BS
    for n, ref in enumerate((x_low, x_high, y_halos.at[0], y_halos.at[1])):

        def one_group(group, carry, ref=ref, n=n):
            rows = [ref[group * count + r] for r in range(count)]
            at = pl.multiple_of(n * piece_len + group * depth, 128)
            for k, piece in enumerate(block_transpose(rows, count, lanes)):
                held[dest_ref[k], :, pl.ds(at, depth)] = piece
            return carry

        lax.fori_loop(0, row_count // count, one_group, 0)
    for k in range(count):
        low = before_z[...] if k == 0 else z_low[k]
        high = after_z[...] if k == count - 1 else z_high[k]
        held[dest_ref[k], :, pl.ds(4 * piece_len, piece_len)] = low
        held[dest_ref[k], :, pl.ds(5 * piece_len, piece_len)] = high
    copies = []
    for d in range(count):
        length = held.shape[2]
        at = pl.ds(0 if outs[d].shape[1] == length else start, length)
        copies.append(pltpu.make_async_copy(held.at[d], outs[d].at[:, at], sems.at[d]))
        copies[d].start()
    for copy in copies:
        copy.wait()


def axis_terms(lower, center, upper):
    ahead = (upper - center) * 0.5
    behind = (center - lower) * 0.5
    second = (ahead - behind) * 0.5
    spread = (
        jnp.abs(ahead)
        + jnp.abs(behind)
        + filter_weight * (jnp.abs(upper) + 2.0 * jnp.abs(center) + jnp.abs(lower))
        + base_term
    )
    return (second * second, spread * spread)


def indicator_kernel(
    prev_ref, rows_ref, next_ref, y_low, y_high, before_z, after_z, *refs
):
    out_ref, held = refs[-2:]
    wide, side_y, count_f, depth = rows_ref.shape
    lanes = lax.broadcasted_iota(jnp.int32, (count_f, depth), 1)
    held[0:WIDTH] = prev_ref[...]
    held[WIDTH : WIDTH + wide] = rows_ref[...]
    held[WIDTH + wide :] = next_ref[...]

    def one_x(x, carry):
        shift = lax.rem(depth - x * (side_y * WIDTH), depth)
        before = pltpu.roll(before_z[...], shift, 1)
        after = pltpu.roll(after_z[...], shift, 1)
        for y in range(side_y):
            center = held[x + WIDTH, y]
            num, den = axis_terms(held[x, y], center, held[x + 2 * WIDTH, y])
            behind = y_low[x, y] if y < WIDTH else held[x + WIDTH, y - WIDTH]
            past = y + WIDTH - side_y
            ahead = y_high[x, past] if past >= 0 else held[x + WIDTH, y + WIDTH]
            num_y, den_y = axis_terms(behind, center, ahead)
            behind = jnp.where(
                lanes < WIDTH,
                pltpu.roll(before, depth - WIDTH * y, 1) if y else before,
                pltpu.roll(center, WIDTH, 1),
            )
            ahead = jnp.where(
                lanes >= depth - WIDTH,
                pltpu.roll(after, depth - WIDTH - WIDTH * y, 1),
                pltpu.roll(center, depth - WIDTH, 1),
            )
            num_z, den_z = axis_terms(behind, center, ahead)
            ratio = (num + num_y + num_z) / (den + den_y + den_z)
            out_ref[x, pl.ds(y, 1), :] = jnp.sqrt(jnp.max(ratio, axis=0, keepdims=True))
        return carry

    lax.fori_loop(0, wide, one_x, 0)


def place_kernel(count, has_base, *refs):
    arrays = refs[:count]
    out, slots = refs[count + has_base : count + has_base + 2]
    held, sems = refs[-count - 1 : -1], refs[-1]
    fetches = [pltpu.make_async_copy(arrays[n], held[n], sems.at[0, n]) for n in range(count)]
    for fetch in fetches:
        fetch.start()
    copies = []
    for n in range(count):
        length = arrays[n].shape[1] - TAIL
        fetches[n].wait()
        slot = jnp.max(held[n][:, pl.ds(length, TAIL)]).astype(jnp.int32)
        slots[n] = slot
        at = pl.ds(0, length)
        copies.append(
            pltpu.make_async_copy(held[n].at[:, at], out.at[slot, :, at], sems.at[1, n])
        )
        copies[n].start()
    for copy in copies:
        copy.wait()


def place(arrays, shape, base=None):
    count = len(arrays)
    has_base = 0 if base is None else 1
    hbm = pl.BlockSpec(memory_space=pltpu.HBM)
    return pl.pallas_call(
        functools.partial(place_kernel, count, has_base),
        out_shape=[
            jax.ShapeDtypeStruct(shape, jnp.float32),
            jax.ShapeDtypeStruct((count,), jnp.int32),
        ],
        in_specs=[pl.BlockSpec(memory_space=pl.ANY)] * count + [hbm] * has_base,
        out_specs=[hbm, pl.BlockSpec(memory_space=pltpu.SMEM)],
        scratch_shapes=[pltpu.VMEM(array.shape, jnp.float32) for array in arrays]
        + [pltpu.SemaphoreType.DMA((2, count))],
        input_output_aliases={count: 0} if has_base else {},
        compiler_params=pltpu.CompilerParams(vmem_limit_bytes=60 * 2**20),
    )(*arrays, *([base] if has_base else []))


def place_halos_kernel(start, count, slots_ref, *refs):
    arrays = refs[:count]
    out, sems = refs[count + 1 :]
    length = arrays[0].shape[1]
    copies = [
        pltpu.make_async_copy(arrays[n], out.at[slots_ref[n], :, pl.ds(start, length)], sems.at[n])
        for n in range(count)
    ]
    for copy in copies:
        copy.start()
    for copy in copies:
        copy.wait()


def place_halos(start, slots, arrays, placed):
    count = len(arrays)
    hbm = pl.BlockSpec(memory_space=pltpu.HBM)
    return pl.pallas_call(
        functools.partial(place_halos_kernel, start, count),
        out_shape=jax.ShapeDtypeStruct(placed.shape, jnp.float32),
        in_specs=[pl.BlockSpec(memory_space=pltpu.SMEM)]
        + [pl.BlockSpec(memory_space=pltpu.VMEM)] * count
        + [hbm],
        out_specs=hbm,
        scratch_shapes=[pltpu.SemaphoreType.DMA((count,))],
        input_output_aliases={1 + count: 0},
        compiler_params=pltpu.CompilerParams(vmem_limit_bytes=12 * 2**20),
    )(slots, *arrays, placed)


def send_order(width_x, width_z):
    xs = [0, 3, 1, 2] if width_x == 4 else list(range(width_x))
    half = width_z // 2
    far = [x * width_z + z for x in xs for z in reversed(range(half, width_z))]
    near = [x * width_z + z for x in reversed(range(width_x)) for z in reversed(range(half))]
    return far, [d for d in near if d]


def interleave(first, second):
    both = []
    while first or second:
        both += first[:1] + second[:1]
        first, second = first[1:], second[1:]
    return both


def ring(axis, move):
    size = lax.axis_size(axis)
    return [(i, (i + move) % size) for i in range(size)]


def per_device(fields, new_owner, new_slot):
    count_f, side_x, side_y, depth = fields.shape
    count = depth // BS
    width_x, width_z = lax.axis_size("gx"), lax.axis_size("gz")
    size = width_x * width_z
    is_power = size & (size - 1) == 0
    me = lax.axis_index(GROUP).astype(jnp.int32)
    dest = offset_of(new_owner.reshape(count), me, size)

    far, near = send_order(width_x, width_z)
    split = far[:AHEAD]
    core_len = side_x * side_y * BS
    halo_len = 12 * BS * side_y
    wide = 4
    part = wide * side_y * BS
    halo_rows = WIDTH * side_y
    row_shape = jax.ShapeDtypeStruct((halo_rows, count_f, depth), jnp.float32)
    hbm = pl.BlockSpec(memory_space=pltpu.HBM)
    whole = pl.BlockSpec(memory_space=pltpu.VMEM)
    *core, x_first, x_last, y_ends = pl.pallas_call(
        functools.partial(core_kernel, wide),
        out_shape=[
            jax.ShapeDtypeStruct(
                (count_f, core_len + (0 if d in split else halo_len) + TAIL), jnp.float32
            )
            for d in range(count)
        ]
        + [row_shape] * 2
        + [jax.ShapeDtypeStruct((2,) + row_shape.shape, jnp.float32)],
        in_specs=[hbm, hbm, hbm],
        out_specs=[hbm] * count + [whole] * 3,
        scratch_shapes=[
            pltpu.VMEM(fields.shape, jnp.float32),
            pltpu.VMEM((2, count, count_f, part), jnp.float32),
            pltpu.VMEM((count, count_f, TAIL), jnp.float32),
            pltpu.SMEM(new_owner.shape, jnp.int32),
            pltpu.SMEM(new_owner.shape, jnp.int32),
            pltpu.SemaphoreType.DMA((side_x // wide,)),
            pltpu.SemaphoreType.DMA((2,)),
            pltpu.SemaphoreType.DMA((3, count)),
        ],
        compiler_params=pltpu.CompilerParams(vmem_limit_bytes=60 * 2**20),
        cost_estimate=pl.CostEstimate(flops=0, bytes_accessed=32 * 2**20, transcendentals=0),
    )(fields, new_owner, new_slot)

    span = 8
    z_shape = jax.ShapeDtypeStruct((count, count_f, halo_rows * BS), jnp.float32)
    edge_shape = jax.ShapeDtypeStruct((count_f, halo_rows * BS), jnp.float32)
    z_block = pl.BlockSpec((count, count_f, depth), lambda i: (0, 0, i))
    edge_block = pl.BlockSpec((count_f, depth), lambda i: (0, i))
    rows_block = pl.BlockSpec((span, side_y, count_f, depth), lambda i: (i, 0, 0, 0))
    rows, z_low, z_high, z_first, z_last = pl.pallas_call(
        edge_kernel,
        out_shape=[
            jax.ShapeDtypeStruct((side_x, side_y, count_f, depth), jnp.float32),
            z_shape,
            z_shape,
            edge_shape,
            edge_shape,
        ],
        grid=(side_x // span,),
        in_specs=[pl.BlockSpec((count_f, span, side_y, depth), lambda i: (0, i, 0, 0))],
        out_specs=[rows_block, z_block, z_block, edge_block, edge_block],
        scratch_shapes=[pltpu.VMEM((count, count_f, depth), jnp.float32)] * 2,
        compiler_params=pltpu.CompilerParams(vmem_limit_bytes=60 * 2**20),
        cost_estimate=pl.CostEstimate(flops=0, bytes_accessed=32 * 2**20, transcendentals=0),
    )(fields)

    values = {("core", d): core[d] for d in split}
    values |= {"x_up": x_last, "x_down": x_first}
    values |= {"z_up": z_last, "z_down": z_first}
    arrived = {}

    def start(name, *after):
        value = values[name]
        if after:
            value, *_ = lax.optimization_barrier((value, *after))
        if isinstance(name, str):
            axis = "g" + name[0]
            pairs = ring(axis, 1 if name.endswith("up") else -1)
        else:
            axis, d = GROUP, name[1]
            move = (lambda s: s ^ d) if is_power else (lambda s: (s + d) % size)
            pairs = [(s, move(s)) for s in range(size)]
        arrived[name] = lax.ppermute(value, axis, pairs)

    far_chain, near_chain = [], []

    def start_far(name, *after):
        past = [arrived[far_chain[-FAR_WINDOW]]] if len(far_chain) >= FAR_WINDOW else []
        start(name, *past, *after)
        far_chain.append(name)

    def start_near(name, *after):
        past = [arrived[near_chain[-NEAR_WINDOW]]] if len(near_chain) >= NEAR_WINDOW else []
        start(name, *past, *after)
        near_chain.append(name)

    for d in split:
        start_far(("core", d))
    start_near("x_up")
    if lax.axis_size("gy") == 2:
        values["y_up"] = y_ends
        start_near("y_up")
        y_halos = arrived["y_up"]
    else:
        values |= {"y_up": y_ends[0], "y_down": y_ends[1]}
        start_near("y_up")
        start_near("y_down")
        y_halos = jnp.stack([arrived["y_up"], arrived["y_down"]])
    start_near("x_down")
    start_near("z_up")
    start_near("z_down")
    x_low, x_high = arrived["x_up"], arrived["x_down"]
    before_z, after_z = arrived["z_up"], arrived["z_down"]

    sequence = interleave(far[AHEAD:] + split, near) + [0]
    full = [d for d in sequence if d not in split]
    halos = pl.pallas_call(
        functools.partial(halo_kernel, core_len, sequence),
        out_shape=[
            jax.ShapeDtypeStruct((count_f, halo_len) if d in split else core[d].shape, jnp.float32)
            for d in sequence
        ],
        in_specs=[pl.BlockSpec(memory_space=pltpu.SMEM)] + [whole] * 7 + [hbm] * len(full),
        out_specs=[hbm] * count,
        input_output_aliases={8 + n: sequence.index(d) for n, d in enumerate(full)},
        scratch_shapes=[
            pltpu.VMEM((count, count_f, halo_len), jnp.float32),
            pltpu.SemaphoreType.DMA((count,)),
        ],
        compiler_params=pltpu.CompilerParams(vmem_limit_bytes=60 * 2**20),
        cost_estimate=pl.CostEstimate(flops=0, bytes_accessed=32 * 2**20, transcendentals=0),
    )(
        dest, x_low, x_high, y_halos, z_low, z_high, before_z, after_z,
        *[core[d] for d in full],
    )
    parts = side_x // span
    per_span = span // WIDTH
    side_block = (WIDTH, side_y, count_f, depth)
    indicators = []
    for n in range(parts):

        def at(block, *index):
            return pl.BlockSpec(block, lambda i: index)

        prev, prev_at = (rows, n * per_span - 1) if n else (x_low.reshape(side_block), 0)
        last = n == parts - 1
        next, next_at = (x_high.reshape(side_block), 0) if last else (rows, (n + 1) * per_span)
        y_block = (None, span, WIDTH, count_f, depth)
        z_part = at((count_f, depth), 0, n)
        indicators.append(
            pl.pallas_call(
                indicator_kernel,
                out_shape=jax.ShapeDtypeStruct((side_x, side_y, depth), jnp.float32),
                grid=(1,),
                in_specs=[
                    at(side_block, prev_at, 0, 0, 0),
                    at((span, side_y, count_f, depth), n, 0, 0, 0),
                    at(side_block, next_at, 0, 0, 0),
                    at(y_block, 0, n, 0, 0, 0),
                    at(y_block, 1, n, 0, 0, 0),
                    z_part,
                    z_part,
                ]
                + [hbm] * (n > 0),
                out_specs=at((span, side_y, depth), n, 0, 0),
                scratch_shapes=[
                    pltpu.VMEM((span + 2 * WIDTH, side_y, count_f, depth), jnp.float32)
                ],
                input_output_aliases={7: 0} if n else {},
                compiler_params=pltpu.CompilerParams(vmem_limit_bytes=60 * 2**20),
                cost_estimate=pl.CostEstimate(
                    flops=10**8, bytes_accessed=16 * 2**20, transcendentals=0
                ),
            )(
                prev,
                rows,
                next,
                y_halos.reshape(2, side_x, WIDTH, count_f, depth),
                y_halos.reshape(2, side_x, WIDTH, count_f, depth),
                before_z,
                after_z,
                *indicators[-1:],
            )
        )

    halos = {d: halos[n] for n, d in enumerate(sequence)}
    values |= {("halo" if d in split else "all", d): halos[d] for d in sequence}
    far_rest = [("all", d) for d in far[AHEAD:]] + [("halo", d) for d in split]
    beside = dict(zip(far_rest[len(far_rest) - parts - len(split) + 1 :], indicators))
    shape = (count, count_f, core_len + halo_len)
    placed, slots = place([arrived["core", d] for d in split], shape)
    beside[far_rest[-len(split) // 2]] = slots
    for name in far_rest:
        start_far(name, *([beside[name]] if name in beside else []))
    for d in near:
        start_near(("all", d))
    placed, _ = place([halos[0]] + [arrived["all", d] for d in full if d], shape, placed)
    placed = place_halos(core_len, slots, [arrived["halo", d] for d in split], placed)
    return (indicators[-1], placed.reshape((1, 1) + shape))


def solution(mesh):
    placed = (P(None, "gx", "gy", "gz"), P("gx", "gy", "gz"), P("gx", "gy", "gz"))
    return jax.shard_map(
        per_device,
        mesh=mesh,
        in_specs=placed,
        out_specs=(P("gx", "gy", "gz"), P("gx", "gy", "gz", None, None)),
        check_vma=False,
    )
```
